32 devices in a mesh: groups: 2 (over y), seq: 4 (over z), head: 2 (over x), sub: 2 (over core).
Axes of the slice: x: 2, y: 2, z: 4, core: 2. Of those that a mesh axis runs over, the one named last changes fastest.
Arguments:
- queries: bfloat16 [6144, 3072], P(('groups', 'seq', 'sub'), 'head'), parts along dimension 0, may hold values from -6 to 6
- keys: bfloat16 [6144, 3072], P(('groups', 'seq', 'sub'), 'head'), parts along dimension 0, may hold values from -6 to 6
- values: bfloat16 [6144, 3072], P(('groups', 'seq', 'sub'), 'head'), parts along dimension 0, may hold values from -6 to 6
- kv_list: int32 [16, 6], P(('groups', 'seq', 'sub')), parts along dimension 0, may hold values from -1 to 7, as said below
- kv_count: int32 [16], P(('groups', 'seq', 'sub')), parts along dimension 0, may hold values from 1 to 6, as said below
- out_weight: bfloat16 [3072, 3072], P('head'), may hold values from -0.5 to 0.5
- gate: float32 [3072], P('head'), may hold values from 1 to 4
Outputs:
- layer_out: bfloat16 [6144, 3072], P(('groups', 'seq', 'sub'), 'head'), parts along dimension 0
The draws below stay inside these ranges and needn't reach their ends.
There are 2 independent parts, one for each index of `groups`. The reference program is written for one: setup_inputs(seed, part) draws one part's arguments, and reference() takes and returns one part's arrays. A program takes and returns all parts, laid end to end along the dimension named above; an argument that names none is the same for every part. Nothing has to cross between parts.
Inputs may be any that keep to these rules, and one draw needn't show every extreme that they name: `kv_list`: tile t lies at time t // 2 and height t % 2 of a slab of 4 x 2 x 1 tiles. Row t begins with t itself, then lists in a drawn order the other tiles of t's 3 x 3 x 3 window clipped to the slab (time within one of t's), then -1 in the entries left over. `kv_count`: at most the number of tiles in the row's clipped window; some tile has 6 and some tile has 1.
All inputs are finite; a program needn't handle non-finite values.
Results may differ from the reference program's by a relative error of at most 0.014.
Values may be sent and summed in bfloat16 or wider, within the bound.
No kernel may reach another device: no remote copies, remote signals or barrier semaphores. Data moves between devices by JAX's collectives and lax.ppermute only.
A program may use at most 128 MiB of HBM per device.

```python
import math
import jax
import jax.numpy as jnp
from jax import lax

HEADS = 24
HD = 128
D = 3072
TILE = 384
WIN = 6
TILES = 8
TOKENS = 3072
N_HEAD = 2


def drawn_field(key, which_one):
    shape = (TILES, TILE, HEADS * HD)
    field = jnp.clip(1.5 * jax.random.normal(jax.random.fold_in(key, 11 + which_one), shape, jnp.float32), -6.0, 6.0)
    return field.reshape(TOKENS, HEADS * HD).astype(jnp.bfloat16)


def draw_queries(key, part):
    return drawn_field(key, 0)


def draw_keys(key, part):
    return drawn_field(key, 1)


def window_lists(key):
    tile_ids = jnp.arange(TILES, dtype=jnp.int32)
    times = tile_ids // 2
    eligible = (jnp.abs(times[:, None] - times[None, :]) <= 1) & (tile_ids[:, None] != tile_ids[None, :])
    noise = jax.random.randint(jax.random.fold_in(key, 31), (TILES, TILES), 0, 65536)
    ranking = jnp.where(eligible, noise * TILES + tile_ids[None, :] + 1, 0)
    scored, picked = lax.top_k(ranking, WIN - 1)
    others = jnp.where(scored > 0, picked.astype(jnp.int32), -1)
    lists = jnp.concatenate([tile_ids[:, None], others], axis=1)
    window_size = 1 + jnp.sum(eligible.astype(jnp.int32), axis=1)
    raw_drops = jax.random.randint(jax.random.fold_in(key, 32), (TILES,), 0, 65536)
    counts = window_size - raw_drops % (window_size // 2 + 1)
    busiest = jax.random.randint(jax.random.fold_in(key, 34), (), 2, TILES - 2)
    corner = jax.random.randint(jax.random.fold_in(key, 35), (), 0, 4)
    lonely = jnp.where(corner < 2, corner, TILES - 4 + corner)
    counts = jnp.where(tile_ids == busiest, WIN, counts)
    counts = jnp.where(tile_ids == lonely, 1, counts)
    return (lists.astype(jnp.int32), counts.astype(jnp.int32))


def draw_kv_list(key, part):
    return window_lists(key)[0]


def draw_kv_count(key, part):
    return window_lists(key)[1]


def block_levels(key, dims, shards, smallest, largest):
    def one(dim, blocks):
        heights = jax.random.uniform(jax.random.fold_in(jax.random.fold_in(key, 6), dim), (blocks,), jnp.float32, smallest / len(shards), largest / len(shards))
        return jnp.repeat(jnp.exp(heights), dims[dim] // blocks).reshape((-1,) + (1,) * (len(dims) - dim - 1))

    level = one(*shards[0])
    for cut in shards[1:]:
        level = level * one(*cut)
    return level


def normal_values(stream_key, shape, spread, bound, pieces=(), held_as=jnp.bfloat16):
    level = block_levels(stream_key, shape, pieces, -0.22, 0.18) if pieces else 1.0
    values = jax.random.normal(stream_key, shape, jnp.float32) * spread * level
    return jnp.minimum(jnp.maximum(values, -bound), bound).astype(held_as)


def setup_inputs(seed: int = 0, part: int = 0) -> dict:
    arg_keys = jax.random.split(jax.random.key(seed), 8)
    part_keys = jax.random.split(jax.random.fold_in(arg_keys[7], part), 8)
    return {
        "queries": draw_queries(jax.random.fold_in(jax.random.fold_in(arg_keys[7], part), 71), part),
        "keys": draw_keys(jax.random.fold_in(jax.random.fold_in(arg_keys[7], part), 71), part),
        "values": normal_values(part_keys[2], (TOKENS, D), 1.0, 6.0, ((0, 8), (1, 2))),
        "kv_list": draw_kv_list(jax.random.fold_in(jax.random.fold_in(arg_keys[7], part), 71), part),
        "kv_count": draw_kv_count(jax.random.fold_in(jax.random.fold_in(arg_keys[7], part), 71), part),
        "out_weight": normal_values(arg_keys[5], (D, D), HD ** -0.5, 0.5, ((0, 2),)),
        "gate": jnp.clip(jnp.exp(math.log(4.0) - 1.3862944 * jax.random.uniform(arg_keys[6], (D,), jnp.float32) ** block_levels(arg_keys[6], (D,), ((0, 2),), -0.2, 0.2)), 1.0, 4.0),
    }


NEG_FILL = -1e+30

def reference(queries, keys, values, kv_list, kv_count, out_weight, gate):
    heads_all = queries.shape[1] // HD
    query_tiles = queries.reshape(TILES, TILE, heads_all, HD)
    key_tiles = keys.reshape(TILES, TILE, heads_all, HD)
    value_tiles = values.reshape(TILES, TILE, heads_all, HD)
    score_scale = 1.0 / math.sqrt(HD)

    def one_tile(tile_index):
        listed = jnp.maximum(kv_list[tile_index], 0).astype(jnp.int32)
        near_keys = key_tiles[listed].astype(jnp.float32)
        near_values = value_tiles[listed].astype(jnp.float32)
        live = jnp.arange(WIN) < kv_count[tile_index]
        scores = jnp.einsum('qhd,wkhd->hqwk', query_tiles[tile_index].astype(jnp.float32), near_keys) * score_scale
        scores = jnp.where(live[None, None, :, None], scores, NEG_FILL)
        peak = lax.optimization_barrier(jnp.max(scores, axis=(2, 3), keepdims=True))
        weights = jnp.exp(scores - peak)
        total = lax.optimization_barrier(jnp.sum(weights, axis=(2, 3)))
        rounded = lax.optimization_barrier(weights.astype(jnp.bfloat16)).astype(jnp.float32)
        mixed = jnp.einsum('hqwk,wkhd->qhd', rounded, near_values)
        return (mixed / jnp.transpose(total)[:, :, None]).astype(jnp.bfloat16)
    attention = lax.map(one_tile, jnp.arange(TILES)).reshape(TOKENS, D)
    group_width = D // N_HEAD
    grouped = attention.reshape(TOKENS, N_HEAD, group_width)
    weight_groups = out_weight.reshape(N_HEAD, group_width, D)

    def add_group(summed, group_index):
        partial_term = jnp.dot(grouped[:, group_index, :], weight_groups[group_index], preferred_element_type=jnp.float32)
        partial_term = lax.optimization_barrier(partial_term.astype(jnp.bfloat16)).astype(jnp.float32)
        return (summed + partial_term, None)
    projected, _ = lax.scan(add_group, jnp.zeros((TOKENS, D), jnp.float32), jnp.arange(N_HEAD))
    return (projected * gate[None, :]).astype(jnp.bfloat16)
```

```python
import functools
import math

import jax
import jax.numpy as jnp
from jax import lax
from jax.experimental import pallas as pl
from jax.experimental.pallas import tpu as pltpu
from jax.sharding import PartitionSpec as P

HD = 128
LOG2E = 1.4426950408889634
FAR = 1e30
ATTEND_BYTES = 16 * 2**20
SHARES = (4, 4, 4)
SMEM_SPEC = pl.BlockSpec(memory_space=pltpu.SMEM)
VMEM_SPEC = pl.BlockSpec(memory_space=pltpu.VMEM)
HBM_SPEC = pl.BlockSpec(memory_space=pltpu.HBM)
BRIEF = pl.CostEstimate(flops=1, bytes_accessed=1, transcendentals=0)


def head_chunks(heads):
    whole = sum(SHARES)
    edges = sorted({(sum(SHARES[:i]) * heads) // whole for i in range(len(SHARES) + 1)})
    return [(low, high - low) for low, high in zip(edges[:-1], edges[1:])]


def pairing(length, first):
    pairs = [(i, i + 1) for i in range(first, length - 1, 2)]
    return pairs + [(b, a) for a, b in pairs]


def ring(length, distance):
    return [(i, (i + distance) % length) for i in range(length)]


def other_core(block):
    return lax.ppermute(block, "sub", [(0, 1), (1, 0)])


def to_neighbours(block):
    length = lax.axis_size("seq")
    return [lax.ppermute(block, "seq", pairing(length, start)) for start in (0, 1)]


def after(value, *earlier):
    return lax.optimization_barrier((value, *earlier))[0]


def pack_kernel(cuts, place_ref, *refs):
    operands, refs = refs[: cuts[0]], refs[cuts[0] :]
    outputs, sems = refs[:-1], refs[-1]
    copies = []
    for out, runs in zip(outputs, cuts[1]):
        at = 0
        for index, row, column, depth, width in runs:
            if isinstance(column, tuple):
                column = pl.multiple_of(place_ref[column[0]], HD)
            source = operands[index].at[row : row + depth, pl.ds(column, width)]
            copies.append(pltpu.make_async_copy(source, out.at[:, at : at + width], sems.at[len(copies)]))
            at += width
    for copy in copies:
        copy.start()
    for copy in copies:
        copy.wait()


def pack(places, operands, cuts):
    shapes = [
        jax.ShapeDtypeStruct((runs[0][3], sum(run[4] for run in runs)), jnp.bfloat16) for runs in cuts
    ]
    return pl.pallas_call(
        functools.partial(pack_kernel, (len(operands), cuts)),
        in_specs=[SMEM_SPEC] + [HBM_SPEC] * len(operands),
        out_specs=[VMEM_SPEC] * len(shapes),
        out_shape=shapes,
        scratch_shapes=[pltpu.SemaphoreType.DMA((sum(len(runs) for runs in cuts),))],
        cost_estimate=BRIEF,
    )(places, *operands)


def attention_kernel(count, columns, base, merge, tiles_ref, list_ref, live_ref, *refs):
    arrays = max(index for index, _ in columns) + 1
    sources = (len(columns) - 1) // 2
    operands, refs = refs[:arrays], refs[arrays:]
    if merge:
        prior_ref, mass_ref, out = refs
    else:
        out, mass_ref = refs
    scale = LOG2E / math.sqrt(HD)
    live = live_ref[0]

    def included(tile):
        found = False
        for j in range(list_ref.shape[1]):
            found = found | ((list_ref[0, j] == tile) & (j < live))
        return found & (tile >= 0)

    flags = [included(tiles_ref[base + s]) for s in range(sources)]

    def cols(head, first=0):
        return slice(first + head * HD, first + (head + 1) * HD)

    def held(i, head):
        index, first = columns[i]
        return operands[index][:, cols(head, first)]

    def scores(head):
        query = held(0, head)
        return [
            lax.dot_general(
                held(1 + 2 * s, head), query, (((1,), (1,)), ((), ())), preferred_element_type=jnp.float32
            )
            for s in range(sources)
        ]

    def finish(head, logits):
        peak = mass_ref[head : head + 1, :] if merge else None
        for s in range(sources):
            top = jnp.max(logits[s], axis=0, keepdims=True) * scale
            if base + s:
                top = jnp.where(flags[s], top, -FAR)
            peak = top if peak is None else jnp.maximum(peak, top)
        accum = total = None
        for s in range(sources):
            shift = jnp.where(flags[s], peak, FAR) if base + s else peak
            weights = jnp.exp2(logits[s] * scale - shift)
            sum_here = jnp.sum(weights, axis=0, keepdims=True)
            term = lax.dot_general(
                held(2 + 2 * s, head),
                weights.astype(jnp.bfloat16),
                (((0,), (0,)), ((), ())),
                preferred_element_type=jnp.float32,
            )
            total = sum_here if total is None else total + sum_here
            accum = term if accum is None else accum + term
        if merge:
            share = jnp.exp2(mass_ref[head : head + 1, :] - peak)
            accum = accum + share * prior_ref[cols(head), :]
            total = total + share
            out[:, cols(head)] = jnp.transpose(accum * (1.0 / total)).astype(out.dtype)
        else:
            out[cols(head), :] = accum * (1.0 / total)
            mass_ref[head : head + 1, :] = peak + jnp.log2(total)

    logits = scores(0)
    for head in range(count):
        following = scores(head + 1) if head + 1 < count else None
        finish(head, logits)
        logits = following


def attend(count, columns, base, scalars, operands, prior=None):
    rows = operands[0].shape[0]
    merge = prior is not None
    sources = (len(columns) - 1) // 2
    whole = jax.ShapeDtypeStruct((rows, count * HD), jnp.bfloat16)
    alone = [
        jax.ShapeDtypeStruct((count * HD, rows), jnp.float32),
        jax.ShapeDtypeStruct((-(-count // 8) * 8, rows), jnp.float32),
    ]
    return pl.pallas_call(
        functools.partial(attention_kernel, count, columns, base, merge),
        in_specs=[SMEM_SPEC] * 3 + [VMEM_SPEC] * (len(operands) + (2 if merge else 0)),
        out_specs=VMEM_SPEC if merge else [VMEM_SPEC] * 2,
        out_shape=whole if merge else alone,
        compiler_params=pltpu.CompilerParams(vmem_limit_bytes=ATTEND_BYTES),
        cost_estimate=BRIEF,
    )(*scalars, *operands, *(prior or ()))


def project_kernel(parts, splits, place_ref, mine_ref, *refs):
    *refs, out = refs
    block = out.shape[1] // splits
    for j in range(splits):
        where = pl.ds(pl.multiple_of(place_ref[j] * block, HD), block)
        total = None
        at = 0
        for i, (chunks, pieces) in enumerate(parts):
            row = 0
            for chunk in refs[at : at + chunks]:
                rows = slice(row, row + chunk.shape[1])
                right = refs[at + chunks + j][rows, :] if i else mine_ref[rows, where]
                term = jnp.dot(chunk[...], right, preferred_element_type=jnp.float32)
                total = term if total is None else total + term
                row += chunk.shape[1]
            at += chunks + pieces
        out[:, where] = total


def project(places, splits, mine, parts):
    operands = [mine]
    for lefts, rights in parts:
        operands += [*lefts, *rights]
    return pl.pallas_call(
        functools.partial(project_kernel, [(len(a), len(b)) for a, b in parts], splits),
        in_specs=[SMEM_SPEC] + [VMEM_SPEC] * len(operands),
        out_specs=VMEM_SPEC,
        out_shape=jax.ShapeDtypeStruct((parts[0][0][0].shape[0], mine.shape[1]), jnp.float32),
        compiler_params=pltpu.CompilerParams(vmem_limit_bytes=ATTEND_BYTES),
        cost_estimate=BRIEF,
    )(places, *operands)


def close_kernel(splits, place_ref, gate_ref, total_ref, *refs):
    *refs, out = refs
    block = out.shape[1] // splits
    for j in range(splits):
        where = pl.ds(pl.multiple_of(place_ref[j] * block, HD), block)
        total = total_ref[:, where]
        for i in range(0, len(refs), 1 + splits):
            total = total + jnp.dot(refs[i][...], refs[i + 1 + j][...], preferred_element_type=jnp.float32)
        out[:, where] = (total * gate_ref[:, where]).astype(out.dtype)


def close(places, splits, gate, total, parts):
    operands = [gate, total]
    for left, rights in parts:
        operands += [left, *rights]
    rows, width = total.shape
    return pl.pallas_call(
        functools.partial(close_kernel, splits),
        in_specs=[SMEM_SPEC] + [VMEM_SPEC] * len(operands),
        out_specs=VMEM_SPEC,
        out_shape=jax.ShapeDtypeStruct((rows, width), jnp.bfloat16),
        compiler_params=pltpu.CompilerParams(vmem_limit_bytes=ATTEND_BYTES),
        cost_estimate=BRIEF,
    )(places, *operands)


def local(queries, keys, values, kv_list, kv_count, out_weight, gate):
    features = queries.shape[1]
    length, subs = lax.axis_size("seq"), lax.axis_size("sub")
    n_head, n_groups = lax.axis_size("head"), lax.axis_size("groups")
    z, c = lax.axis_index("seq"), lax.axis_index("sub")
    x, g = lax.axis_index("head"), lax.axis_index("groups")
    width = out_weight.shape[1] // n_head
    chunks = head_chunks(features // HD)
    last = len(chunks) - 1
    spans = [slice(first * HD, (first + count) * HD) for first, count in chunks]

    even = z + 1 - 2 * lax.rem(z, 2)
    odd = z - 1 + 2 * lax.rem(z, 2)
    tiles = []
    for place in (z, even, odd):
        inside = (place >= 0) & (place < length)
        tiles += [jnp.where(inside, place * subs + c, -1), jnp.where(inside, place * subs + 1 - c, -1)]
    scalars = (jnp.stack(tiles).astype(jnp.int32), kv_list, kv_count)

    splits = n_groups * subs
    if width % (splits * HD):
        splits = 1
    block = width // splits
    if splits > 1:
        places = [lax.rem(g + d, n_groups) * subs + s for d in range(n_groups) for s in (c, 1 - c)]
    else:
        places = [0]
    piece = places[0]
    places = jnp.stack(places).astype(jnp.int32)
    edges = [0, chunks[last][0] * HD, features]

    def cross(sent):
        return [lax.ppermute(block, "head", ring(n_head, d + 1)) for d, block in enumerate(sent)]

    def spread(got):
        if splits == 1:
            return [got]
        found = []
        for e in range(n_groups):
            near = got if e == 0 else lax.ppermute(got, "groups", ring(n_groups, n_groups - e))
            found += [near, other_core(near)]
        return found

    def along_head(done):
        return [lax.ppermute(done, "head", ring(n_head, d)) for d in range(1, n_head)]

    starts = [lax.rem(x + d, n_head) * width + piece * block for d in range(1, n_head)]
    starts = jnp.stack([x * width, *starts]).astype(jnp.int32)

    def pair_cut(i):
        first, count = chunks[i]
        return tuple((index, 0, first * HD, keys.shape[0], count * HD) for index in (0, 1))

    def weight_cut(part, d):
        return ((2, edges[part], (d,), edges[part + 1] - edges[part], block),)

    blocks = list(pack(starts, (keys, values), (pair_cut(0),)))
    near = [to_neighbours(blocks[0])]
    sib_keys, sib_values = other_core(keys), other_core(values)
    cuts = [pair_cut(i) for i in range(1, len(chunks))]
    cuts += [weight_cut(part, d) for part in (0, 1) for d in range(1, n_head)]
    cuts.append(((2, 0, (0,), features, width),))
    packed = list(pack(starts, (keys, values, out_weight), tuple(cuts)))
    sib_keys, sib_values, packed = lax.optimization_barrier((sib_keys, sib_values, packed))
    blocks += packed[:last]
    sent, mine = packed[last:-1], packed[-1]
    near.append(to_neighbours(blocks[1]))
    crossed = [cross(sent[: n_head - 1])]

    prior = []
    for first, count in chunks:
        at = first * HD
        columns = tuple((index, at) for index in range(5))
        prior.append(attend(count, columns, 0, scalars, (queries, keys, values, sib_keys, sib_values)))
    near[0] = list(lax.optimization_barrier((near[0], prior))[0])

    crossed.append(cross(after(sent[n_head - 1 :], crossed[0])))
    mixed, moved = [], []
    for i, (first, count) in enumerate(chunks):
        fetched = []
        for part in near[i]:
            fetched += [part, other_core(part)]
        columns = [(0, first * HD)]
        for index in range(len(fetched)):
            columns += [(1 + index, 0), (1 + index, count * HD)]
        done = attend(count, tuple(columns), 2, scalars, (queries, *fetched), prior[i])
        if i + 2 < len(chunks):
            near.append(to_neighbours(after(blocks[i + 2], done, crossed[1])))
        if i + 1 < len(chunks):
            near[i + 1] = list(after(near[i + 1], done))
        mixed.append(done)
        moved.append(along_head(done))

    pieces = [[spread(got) for got in crossed[part]] for part in (0, 1)]
    parts = [(mixed, [])]
    parts += [([moved[i][d] for i in range(last)], pieces[0][d]) for d in range(n_head - 1)]
    total = project(places, splits, mine, parts)
    parts = [(moved[last][d], pieces[1][d]) for d in range(n_head - 1)]
    return close(places, splits, gate.reshape(1, width), total, parts)


def solution(mesh):
    return jax.shard_map(
        local,
        mesh=mesh,
        in_specs=(
            P(("groups", "seq", "sub"), "head"),
            P(("groups", "seq", "sub"), "head"),
            P(("groups", "seq", "sub"), "head"),
            P(("groups", "seq", "sub"), None),
            P(("groups", "seq", "sub")),
            P("head", None),
            P("head"),
        ),
        out_specs=P(("groups", "seq", "sub"), "head"),
        check_vma=False,
    )
```

```python
import functools
import math

import jax
import jax.numpy as jnp
from jax import lax
from jax.experimental import pallas as pl
from jax.experimental.pallas import tpu as pltpu
from jax.sharding import PartitionSpec as P

HD = 128
LOG2E = 1.4426950408889634
FAR = 1e30
KERNEL_BYTES = 12 * 2**20
PROJECT_BYTES = 12 * 2**20
PACK_BYTES = 56 * 2**20
SHARES = (2, 2, 2)
SMEM_SPEC = pl.BlockSpec(memory_space=pltpu.SMEM)
VMEM_SPEC = pl.BlockSpec(memory_space=pltpu.VMEM)
HBM_SPEC = pl.BlockSpec(memory_space=pltpu.HBM)


def head_chunks(heads):
    whole = sum(SHARES)
    edges = sorted({(sum(SHARES[:i]) * heads) // whole for i in range(len(SHARES) + 1)})
    return [(low, high - low) for low, high in zip(edges[:-1], edges[1:])]


def pairing(length, first):
    pairs = [(i, i + 1) for i in range(first, length - 1, 2)]
    return pairs + [(b, a) for a, b in pairs]


def ring(length, distance):
    return [(i, (i + distance) % length) for i in range(length)]


def other_core(block):
    return lax.ppermute(block, "sub", [(0, 1), (1, 0)])


def to_neighbours(block):
    length = lax.axis_size("seq")
    return [lax.ppermute(block, "seq", pairing(length, start)) for start in (0, 1)]


def after(value, *earlier):
    return lax.optimization_barrier((value, *earlier))[0]


def pack_kernel(inputs, cuts, *refs):
    operands, outputs, sems = refs[:inputs], refs[inputs:-1], refs[-1]
    copies = []
    for out, runs in zip(outputs, cuts):
        at = 0
        for index, start_of, offset, width in runs:
            begin = start_of() + offset
            for step in range(0, width, HD):
                start = pl.multiple_of(begin + step, HD)
                copies.append(
                    pltpu.make_async_copy(
                        operands[index].at[:, pl.ds(start, HD)], out.at[:, at : at + HD], sems.at[len(copies)]
                    )
                )
                at += HD
    for copy in copies:
        copy.start()
    for copy in copies:
        copy.wait()


def pack(operands, cuts):
    shapes = [
        jax.ShapeDtypeStruct((operands[runs[0][0]].shape[0], sum(run[3] for run in runs)), jnp.bfloat16)
        for runs in cuts
    ]
    return pl.pallas_call(
        functools.partial(pack_kernel, len(operands), cuts),
        in_specs=[HBM_SPEC] * len(operands),
        out_specs=[VMEM_SPEC] * len(shapes),
        out_shape=shapes,
        scratch_shapes=[pltpu.SemaphoreType.DMA((sum(run[3] // HD for runs in cuts for run in runs),))],
        compiler_params=pltpu.CompilerParams(vmem_limit_bytes=PACK_BYTES),
    )(*operands)


def join_kernel(span, cuts, *refs):
    *operands, found = refs[: -len(cuts)]
    half = lax.axis_index("sub") * span
    for (low, runs), out in zip(cuts, refs[-len(cuts) :]):
        rows, width = found.shape[0], out.shape[1]
        at = 0
        for index, offset, size in runs:
            start = pl.multiple_of(half + offset, HD)
            out[:rows, at : at + size] = operands[index][:, pl.ds(start, size)]
            at += size
        out[rows:, :] = found[:, low : low + width]


def join(operands, found, span, cuts):
    rows = found.shape[0]
    widths = [sum(size for _, _, size in runs) for _, runs in cuts]
    return pl.pallas_call(
        functools.partial(join_kernel, span, cuts),
        in_specs=[VMEM_SPEC] * (len(operands) + 1),
        out_specs=[VMEM_SPEC] * len(cuts),
        out_shape=[jax.ShapeDtypeStruct((2 * rows, width), found.dtype) for width in widths],
        compiler_params=pltpu.CompilerParams(vmem_limit_bytes=PROJECT_BYTES),
    )(*operands, found)


def attention_kernel(first, plan, base, merge, tiles_ref, lists_ref, queries, *refs):
    arrays = max(index for held in plan for index, *_ in held) + 1
    operands, refs = refs[:arrays], refs[arrays:]
    if merge:
        prior_ref, mass_ref, *outs = refs
    else:
        out, mass_ref = refs
    rows = queries.shape[0] // 2
    entries = lists_ref.shape[1] - 1
    scale = LOG2E / math.sqrt(HD)
    early = lax.broadcasted_iota(jnp.int32, (1, 2 * rows), 1) < rows

    def included(query, tile):
        found = False
        for j in range(entries):
            found = found | ((lists_ref[query, j] == tile) & (j < lists_ref[query, entries]))
        return (found & (tile >= 0)).astype(jnp.int32)

    flags = []
    for s in range(len(plan[0])):
        tile = tiles_ref[base + s]
        flags.append(jnp.where(early, included(0, tile), included(1, tile)) > 0)

    def block(index, row, column):
        return operands[index][row : row + rows, column : column + HD]

    def scores(head):
        query = queries[:, (first + head) * HD : (first + head + 1) * HD]
        return [
            lax.dot_general(
                block(index, row, key), query, (((1,), (1,)), ((), ())), preferred_element_type=jnp.float32
            )
            for index, row, key, _ in plan[head]
        ]

    def finish(head, logits):
        cols = slice(head * HD, (head + 1) * HD)
        seen = slice((first + head) * HD, (first + head + 1) * HD)
        peak = before = mass_ref[first + head : first + head + 1, :] if merge else None
        for flag, logit in zip(flags, logits):
            top = jnp.where(flag, jnp.max(logit, axis=0, keepdims=True) * scale, -FAR)
            peak = top if peak is None else jnp.maximum(peak, top)
        accum = total = None
        for (index, row, _, value), flag, logit in zip(plan[head], flags, logits):
            weights = jnp.exp2(logit * scale - jnp.where(flag, peak, FAR))
            mass = jnp.sum(weights, axis=0, keepdims=True)
            term = lax.dot_general(
                block(index, row, value),
                weights.astype(jnp.bfloat16),
                (((0,), (0,)), ((), ())),
                preferred_element_type=jnp.float32,
            )
            total = mass if total is None else total + mass
            accum = term if accum is None else accum + term
        if merge:
            share = jnp.exp2(before - peak)
            accum = accum + share * prior_ref[seen, :]
            total = total + share
            result = accum * (1.0 / total)
            for i, out_i in enumerate(outs):
                out_i[:, cols] = jnp.transpose(result[:, i * rows : (i + 1) * rows]).astype(out_i.dtype)
        else:
            out[cols, :] = accum * (1.0 / total)
            mass_ref[head : head + 1, :] = peak + jnp.log2(total)

    logits = scores(0)
    for head in range(len(plan)):
        following = scores(head + 1) if head + 1 < len(plan) else None
        finish(head, logits)
        logits = following


def attend(first, plan, base, scalars, queries, operands, prior=None):
    rows = queries.shape[0] // 2
    count = len(plan)
    merge = prior is not None
    if merge:
        shapes = [jax.ShapeDtypeStruct((rows, count * HD), jnp.bfloat16)] * 2
    else:
        shapes = [
            jax.ShapeDtypeStruct((count * HD, 2 * rows), jnp.float32),
            jax.ShapeDtypeStruct((-(-count // 8) * 8, 2 * rows), jnp.float32),
        ]
    operands = (queries, *operands, *(prior or ()))
    return pl.pallas_call(
        functools.partial(attention_kernel, first, plan, base, merge),
        in_specs=[SMEM_SPEC] * 2 + [VMEM_SPEC] * len(operands),
        out_specs=[VMEM_SPEC] * 2,
        out_shape=shapes,
        compiler_params=pltpu.CompilerParams(vmem_limit_bytes=KERNEL_BYTES),
    )(*scalars, *operands)


def project_kernel(splits, groups, carried, gated, place_ref, *refs):
    refs = list(refs)
    if gated:
        held, sems = refs.pop(-2), refs.pop(-1)
    out = refs.pop()
    copies = []
    total_ref = refs.pop(0) if carried else None
    gate_ref = refs.pop(0) if gated else None
    block = out.shape[1] // splits
    for j in range(splits):
        where = pl.ds(pl.multiple_of(place_ref[j] * block, HD), block)
        total = total_ref[:, where] if carried else None
        at = 0
        for runs, arrays, pieces in groups:
            weights = refs[at + arrays : at + arrays + max(pieces, 1)]
            for index, column, place, offset, depth in runs:
                rows = pl.ds(pl.multiple_of(place_ref[place] + offset, HD), depth)
                right = weights[j][rows, :] if pieces else weights[0][rows, where]
                left = refs[at + index][:, column : column + depth]
                term = jnp.dot(left, right, preferred_element_type=jnp.float32)
                total = term if total is None else total + term
            at += arrays + max(pieces, 1)
        if gated:
            held[:, j * block : (j + 1) * block] = (total * gate_ref[:, where]).astype(out.dtype)
            source = held.at[:, j * block : (j + 1) * block]
            copies.append(pltpu.make_async_copy(source, out.at[:, where], sems.at[j]))
            copies[-1].start()
        else:
            out[:, where] = total
    for copy in copies:
        copy.wait()


def project(places, splits, groups, width, total=None, gate=None):
    operands = [a for a in (total, gate) if a is not None]
    plan = []
    for runs, arrays, weights, whole in groups:
        plan.append((runs, len(arrays), 0 if whole else len(weights)))
        operands += [*arrays, *weights]
    rows = groups[0][1][0].shape[0]
    scratch = [pltpu.VMEM((rows, width), jnp.bfloat16), pltpu.SemaphoreType.DMA((splits,))]
    return pl.pallas_call(
        functools.partial(project_kernel, splits, plan, total is not None, gate is not None),
        in_specs=[SMEM_SPEC] + [VMEM_SPEC] * len(operands),
        out_specs=VMEM_SPEC if gate is None else HBM_SPEC,
        out_shape=jax.ShapeDtypeStruct((rows, width), jnp.float32 if gate is None else jnp.bfloat16),
        scratch_shapes=scratch if gate is not None else [],
        compiler_params=pltpu.CompilerParams(vmem_limit_bytes=PROJECT_BYTES),
    )(places, *operands)


def local(queries, keys, values, kv_list, kv_count, out_weight, gate):
    rows = queries.shape[0]
    length, subs = lax.axis_size("seq"), lax.axis_size("sub")
    n_head, n_groups = lax.axis_size("head"), lax.axis_size("groups")
    z, c = lax.axis_index("seq"), lax.axis_index("sub")
    x, g = lax.axis_index("head"), lax.axis_index("groups")
    width = out_weight.shape[1] // n_head
    heads = queries.shape[1] // HD
    if heads % 2:
        queries, keys, values = (jnp.pad(a, ((0, 0), (0, HD))) for a in (queries, keys, values))
        out_weight = jnp.pad(out_weight, ((0, HD), (0, 0)))
    half = (heads + 1) // 2
    span = half * HD
    chunks = head_chunks(half)
    last = len(chunks) - 1

    even = z + 1 - 2 * lax.rem(z, 2)
    odd = z - 1 + 2 * lax.rem(z, 2)
    tiles = []
    for place in (z, even, odd):
        inside = (place >= 0) & (place < length)
        tiles += [jnp.where(inside, place * subs + c, -1), jnp.where(inside, place * subs + 1 - c, -1)]
    lists = jnp.concatenate([kv_list, kv_count.reshape(1, 1)], axis=1)

    splits = n_groups * subs
    if width % (splits * HD):
        splits = 1
    block = width // splits
    if splits > 1:
        places = [lax.rem(g + d, n_groups) * subs + s for d in range(n_groups) for s in (c, 1 - c)]
    else:
        places = [0]

    def piece_at(d):
        there = lax.rem(lax.axis_index("head") + d, n_head) * width
        return there + ((lax.axis_index("groups") * subs + lax.axis_index("sub")) * block if splits > 1 else 0)

    piece = places[0]
    places = jnp.stack([*places, c * span, (1 - c) * span]).astype(jnp.int32)

    runs_of = [((2, 0, span),)]
    for first, count in chunks:
        runs_of.append(tuple((index, first * HD, count * HD) for index in (0, 1)))
    cuts, low = [], 0
    for runs in runs_of:
        cuts.append((low, runs))
        low += sum(size for _, _, size in runs)

    def other_half():
        return (1 - lax.axis_index("sub")) * span

    cut = tuple((index, other_half, offset, size) for runs in runs_of for index, offset, size in runs)
    (other,) = pack((keys, values, queries), (cut,))
    found = other_core(other)
    sent = [
        lax.dynamic_slice(out_weight, (0, lax.rem(x + d, n_head) * width + piece * block), (2 * span, block))
        for d in range(1, n_head)
    ]
    first_message = join((keys, values), found, span, cuts[1:2])
    queries, *message = join((keys, values, queries), found, span, [cuts[0], *cuts[2:]])
    message = [*first_message, *message]
    near = [to_neighbours(message[0])]
    lists = jnp.concatenate([lists, other_core(lists)], axis=0)
    scalars = (jnp.stack(tiles).astype(jnp.int32), lists)

    near.append(to_neighbours(message[1]))
    crossed = [lax.ppermute(a, "head", ring(n_head, d + 1)) for d, a in enumerate(sent)]

    def runs(some):
        return [
            (index, side * chunks[i][1] * HD, splits + side, chunks[i][0] * HD, chunks[i][1] * HD)
            for index, i in enumerate(some)
            for side in (0, 1)
        ]

    def plan_of(i, sources):
        count = chunks[i][1]
        return [tuple((a, row, h * HD, (count + h) * HD) for a, row in sources) for h in range(count)]

    plan = sum((plan_of(i, ((i, 0), (i, rows))) for i in range(len(chunks))), [])
    prior = attend(0, plan, 0, scalars, queries, message)
    mine = lax.dynamic_slice(after(out_weight, prior), (0, x * width), (2 * span, width))
    near[0], crossed = lax.optimization_barrier((after(near[0], prior, mine), crossed))
    spread = [
        [got] + [lax.ppermute(got, "groups", ring(n_groups, n_groups - e)) for e in range(1, n_groups)]
        if splits > 1
        else [got]
        for got in crossed
    ]

    ours, moved = [], []
    for i, (first, _) in enumerate(chunks):
        plan = plan_of(i, [(index, row) for index in (0, 1) for row in (0, rows)])
        kept, given = attend(first, plan, 2, scalars, queries, near[i], prior)
        ours.append(jnp.concatenate([kept, other_core(given)], axis=1))
        leaving = after(ours[i], moved) if i else ours[i]
        moved.append([lax.ppermute(leaving, "head", ring(n_head, d)) for d in range(1, n_head)])
        if i + 2 < len(chunks):
            near.append(to_neighbours(after(message[i + 2], kept)))
        if i == 0:
            near[1] = after(near[1], kept, ours[0])
        if i == last - 1:
            total = project(places, splits, [(runs(range(last)), ours[:], [mine], True)], width)
            near[last], spread = lax.optimization_barrier((after(near[last], total, moved), spread))
    pieces = [[a for got in gots for a in (got, other_core(got))] if splits > 1 else gots for gots in spread]

    groups = [(runs([last]), [ours[last]], [mine], True)]
    groups += [(runs(range(last)), [moved[i][d] for i in range(last)], pieces[d], False) for d in range(n_head - 1)]
    total = project(places, splits, groups, width, total)
    groups = [(runs([last]), [moved[last][d]], pieces[d], False) for d in range(n_head - 1)]
    return project(places, splits, groups, width, total, gate.reshape(1, width))


def solution(mesh):
    return jax.shard_map(
        local,
        mesh=mesh,
        in_specs=(
            P(("groups", "seq", "sub"), "head"),
            P(("groups", "seq", "sub"), "head"),
            P(("groups", "seq", "sub"), "head"),
            P(("groups", "seq", "sub"), None),
            P(("groups", "seq", "sub")),
            P("head", None),
            P("head"),
        ),
        out_specs=P(("groups", "seq", "sub"), "head"),
        check_vma=False,
    )
```

```python
import functools
import math

import jax
import jax.numpy as jnp
from jax import lax
from jax.experimental import pallas as pl
from jax.experimental.pallas import tpu as pltpu
from jax.sharding import PartitionSpec as P

HD = 128
LOG2E = 1.4426950408889634
FAR = 1e30
KERNEL_BYTES = 12 * 2**20
PROJECT_BYTES = 12 * 2**20
PACK_BYTES = 56 * 2**20
SHARES = (2, 2, 2)
SMEM_SPEC = pl.BlockSpec(memory_space=pltpu.SMEM)
VMEM_SPEC = pl.BlockSpec(memory_space=pltpu.VMEM)
HBM_SPEC = pl.BlockSpec(memory_space=pltpu.HBM)


def head_chunks(heads):
    whole = sum(SHARES)
    edges = sorted({(sum(SHARES[:i]) * heads) // whole for i in range(len(SHARES) + 1)})
    return [(low, high - low) for low, high in zip(edges[:-1], edges[1:])]


def pairing(length, first):
    pairs = [(i, i + 1) for i in range(first, length - 1, 2)]
    return pairs + [(b, a) for a, b in pairs]


def ring(length, distance):
    return [(i, (i + distance) % length) for i in range(length)]


def other_core(block):
    return lax.ppermute(block, "sub", [(0, 1), (1, 0)])


def to_neighbours(block):
    length = lax.axis_size("seq")
    return [lax.ppermute(block, "seq", pairing(length, start)) for start in (0, 1)]


def after(value, *earlier):
    return lax.optimization_barrier((value, *earlier))[0]


def pack_kernel(inputs, runs, *refs):
    operands, out, held, sems = refs[:inputs], *refs[inputs:]
    arriving, leaving = [], []
    other_half = (1 - lax.axis_index("sub")) * (operands[0].shape[1] // 2)
    for index, offset, width in runs:
        for step in range(0, width, HD):
            n = len(arriving)
            start = pl.multiple_of(other_half + (offset + step), HD)
            place = (slice(None), slice(n * HD, (n + 1) * HD))
            arriving.append(
                pltpu.make_async_copy(operands[index].at[:, pl.ds(start, HD)], held.at[place], sems.at[0, n])
            )
            leaving.append(pltpu.make_async_copy(held.at[place], out.at[place], sems.at[1, n]))
    for copy in arriving:
        copy.start()
    for arrival, departure in zip(arriving, leaving):
        arrival.wait()
        departure.start()
    for copy in leaving:
        copy.wait()


def pack(operands, runs):
    shape = (operands[0].shape[0], sum(width for _, _, width in runs))
    return pl.pallas_call(
        functools.partial(pack_kernel, len(operands), runs),
        in_specs=[HBM_SPEC] * len(operands),
        out_specs=HBM_SPEC,
        out_shape=jax.ShapeDtypeStruct(shape, jnp.bfloat16),
        scratch_shapes=[pltpu.VMEM(shape, jnp.bfloat16), pltpu.SemaphoreType.DMA((2, shape[1] // HD))],
        compiler_params=pltpu.CompilerParams(vmem_limit_bytes=PACK_BYTES),
    )(*operands)


def join_kernel(span, cuts, *refs):
    *operands, found = refs[: -len(cuts)]
    half = lax.axis_index("sub") * span
    for (low, runs), out in zip(cuts, refs[-len(cuts) :]):
        rows, width = found.shape[0], out.shape[1]
        at = 0
        for index, offset, size in runs:
            start = pl.multiple_of(half + offset, HD)
            out[:rows, at : at + size] = operands[index][:, pl.ds(start, size)]
            at += size
        out[rows:, :] = found[:, low : low + width]


def join(operands, found, span, cuts):
    rows = found.shape[0]
    widths = [sum(size for _, _, size in runs) for _, runs in cuts]
    return pl.pallas_call(
        functools.partial(join_kernel, span, cuts),
        in_specs=[VMEM_SPEC] * (len(operands) + 1),
        out_specs=[VMEM_SPEC] * len(cuts),
        out_shape=[jax.ShapeDtypeStruct((2 * rows, width), found.dtype) for width in widths],
        compiler_params=pltpu.CompilerParams(vmem_limit_bytes=PROJECT_BYTES),
    )(*operands, found)


def attention_kernel(first, plan, base, merge, tiles_ref, lists_ref, queries, *refs):
    arrays = max(index for held in plan for index, *_ in held) + 1
    operands, refs = refs[:arrays], refs[arrays:]
    if merge:
        prior_ref, mass_ref, *outs = refs
    else:
        out, mass_ref = refs
    rows = queries.shape[0] // 2
    entries = lists_ref.shape[1] - 1
    scale = LOG2E / math.sqrt(HD)
    early = lax.broadcasted_iota(jnp.int32, (1, 2 * rows), 1) < rows

    def included(query, tile):
        found = False
        for j in range(entries):
            found = found | ((lists_ref[query, j] == tile) & (j < lists_ref[query, entries]))
        return (found & (tile >= 0)).astype(jnp.int32)

    flags = []
    for s in range(len(plan[0])):
        tile = tiles_ref[base + s]
        flags.append(jnp.where(early, included(0, tile), included(1, tile)) > 0)

    def block(index, row, column):
        return operands[index][row : row + rows, column : column + HD]

    def scores(head):
        query = queries[:, (first + head) * HD : (first + head + 1) * HD]
        return [
            lax.dot_general(
                block(index, row, key), query, (((1,), (1,)), ((), ())), preferred_element_type=jnp.float32
            )
            for index, row, key, _ in plan[head]
        ]

    def finish(head, logits):
        cols = slice(head * HD, (head + 1) * HD)
        seen = slice((first + head) * HD, (first + head + 1) * HD)
        peak = before = mass_ref[first + head : first + head + 1, :] if merge else None
        for flag, logit in zip(flags, logits):
            top = jnp.where(flag, jnp.max(logit, axis=0, keepdims=True) * scale, -FAR)
            peak = top if peak is None else jnp.maximum(peak, top)
        accum = total = None
        for (index, row, _, value), flag, logit in zip(plan[head], flags, logits):
            weights = jnp.exp2(logit * scale - jnp.where(flag, peak, FAR))
            mass = jnp.sum(weights, axis=0, keepdims=True)
            term = lax.dot_general(
                block(index, row, value),
                weights.astype(jnp.bfloat16),
                (((0,), (0,)), ((), ())),
                preferred_element_type=jnp.float32,
            )
            total = mass if total is None else total + mass
            accum = term if accum is None else accum + term
        if merge:
            share = jnp.exp2(before - peak)
            accum = accum + share * prior_ref[seen, :]
            total = total + share
            result = accum * (1.0 / total)
            for i, out_i in enumerate(outs):
                out_i[:, cols] = jnp.transpose(result[:, i * rows : (i + 1) * rows]).astype(out_i.dtype)
        else:
            out[cols, :] = accum * (1.0 / total)
            mass_ref[head : head + 1, :] = peak + jnp.log2(total)

    logits = scores(0)
    for head in range(len(plan)):
        following = scores(head + 1) if head + 1 < len(plan) else None
        finish(head, logits)
        logits = following


def attend(first, plan, base, scalars, queries, operands, prior=None):
    rows = queries.shape[0] // 2
    count = len(plan)
    merge = prior is not None
    if merge:
        shapes = [jax.ShapeDtypeStruct((rows, count * HD), jnp.bfloat16)] * 2
    else:
        shapes = [
            jax.ShapeDtypeStruct((count * HD, 2 * rows), jnp.float32),
            jax.ShapeDtypeStruct((-(-count // 8) * 8, 2 * rows), jnp.float32),
        ]
    operands = (queries, *operands, *(prior or ()))
    return pl.pallas_call(
        functools.partial(attention_kernel, first, plan, base, merge),
        in_specs=[SMEM_SPEC] * 2 + [VMEM_SPEC] * len(operands),
        out_specs=[VMEM_SPEC] * 2,
        out_shape=shapes,
        compiler_params=pltpu.CompilerParams(vmem_limit_bytes=KERNEL_BYTES),
    )(*scalars, *operands)


def project_kernel(splits, groups, carried, late, place_ref, *refs):
    refs = list(refs)
    weights_out = refs.pop() if late else None
    out = refs.pop()
    total_ref = refs.pop(0) if carried else None
    block = out.shape[1] // splits
    for j in range(splits):
        where = pl.ds(pl.multiple_of(place_ref[j] * block, HD), block)
        total = total_ref[:, where] if carried else None
        at = row = 0
        for runs, arrays, pieces in groups:
            weights = refs[at + arrays : at + arrays + max(pieces, 1)]
            for index, column, place, offset, depth in runs:
                rows = pl.ds(pl.multiple_of(place_ref[place] + offset, HD), depth)
                right = weights[j][rows, :] if pieces else weights[0][rows, where]
                left = refs[at + index][:, column : column + depth]
                term = jnp.dot(left, right, preferred_element_type=jnp.float32)
                total = term if total is None else total + term
            for place, offset, depth in late if pieces else ():
                rows = pl.ds(pl.multiple_of(place_ref[place] + offset, HD), depth)
                weights_out[row : row + depth, where] = weights[j][rows, :]
                row += depth
            at += arrays + max(pieces, 1)
        out[:, where] = total


def project(places, splits, groups, width, total=None, late=()):
    operands = [] if total is None else [total]
    plan = []
    for runs, arrays, weights, whole in groups:
        plan.append((runs, len(arrays), 0 if whole else len(weights)))
        operands += [*arrays, *weights]
    rows = groups[0][1][0].shape[0]
    shapes = [jax.ShapeDtypeStruct((rows, width), jnp.float32)]
    if late:
        depth = sum(depth for _, _, depth in late) * sum(not whole for *_, whole in groups)
        shapes.append(jax.ShapeDtypeStruct((depth, width), jnp.bfloat16))
    return pl.pallas_call(
        functools.partial(project_kernel, splits, plan, total is not None, late),
        in_specs=[SMEM_SPEC] + [VMEM_SPEC] * len(operands),
        out_specs=[VMEM_SPEC] * len(shapes),
        out_shape=shapes,
        compiler_params=pltpu.CompilerParams(vmem_limit_bytes=PROJECT_BYTES),
    )(places, *operands)


def close_kernel(blocks, total_ref, weights_ref, gate_ref, *refs):
    *parts, out, held, sems = refs
    block = out.shape[1] // blocks
    copies = []
    for j in range(blocks):
        where = slice(j * block, (j + 1) * block)
        total = total_ref[:, where]
        row = 0
        for part in parts:
            depth = part.shape[1]
            right = weights_ref[row : row + depth, where]
            total = total + jnp.dot(part[...], right, preferred_element_type=jnp.float32)
            row += depth
        held[:, where] = (total * gate_ref[:, where]).astype(out.dtype)
        copies.append(pltpu.make_async_copy(held.at[:, where], out.at[:, where], sems.at[j]))
        copies[-1].start()
    for copy in copies:
        copy.wait()


def close(total, weights, parts, gate):
    rows, width = total.shape
    blocks = max(width // (4 * HD), 1)
    return pl.pallas_call(
        functools.partial(close_kernel, blocks),
        in_specs=[VMEM_SPEC] * (3 + len(parts)),
        out_specs=HBM_SPEC,
        out_shape=jax.ShapeDtypeStruct((rows, width), jnp.bfloat16),
        scratch_shapes=[pltpu.VMEM((rows, width), jnp.bfloat16), pltpu.SemaphoreType.DMA((blocks,))],
        compiler_params=pltpu.CompilerParams(vmem_limit_bytes=PROJECT_BYTES),
    )(total, weights, gate, *parts)


def local(queries, keys, values, kv_list, kv_count, out_weight, gate):
    rows = queries.shape[0]
    length, subs = lax.axis_size("seq"), lax.axis_size("sub")
    n_head, n_groups = lax.axis_size("head"), lax.axis_size("groups")
    z, c = lax.axis_index("seq"), lax.axis_index("sub")
    x, g = lax.axis_index("head"), lax.axis_index("groups")
    width = out_weight.shape[1] // n_head
    heads = queries.shape[1] // HD
    if heads % 2:
        queries, keys, values = (jnp.pad(a, ((0, 0), (0, HD))) for a in (queries, keys, values))
        out_weight = jnp.pad(out_weight, ((0, HD), (0, 0)))
    half = (heads + 1) // 2
    span = half * HD
    chunks = head_chunks(half)
    last = len(chunks) - 1

    even = z + 1 - 2 * lax.rem(z, 2)
    odd = z - 1 + 2 * lax.rem(z, 2)
    tiles = []
    for place in (z, even, odd):
        inside = (place >= 0) & (place < length)
        tiles += [jnp.where(inside, place * subs + c, -1), jnp.where(inside, place * subs + 1 - c, -1)]
    lists = jnp.concatenate([kv_list, kv_count.reshape(1, 1)], axis=1)

    splits = n_groups * subs
    if width % (splits * HD):
        splits = 1
    block = width // splits
    if splits > 1:
        places = [lax.rem(g + d, n_groups) * subs + s for d in range(n_groups) for s in (c, 1 - c)]
    else:
        places = [0]

    def piece_at(d):
        there = lax.rem(lax.axis_index("head") + d, n_head) * width
        return there + ((lax.axis_index("groups") * subs + lax.axis_index("sub")) * block if splits > 1 else 0)

    piece = places[0]
    places = jnp.stack([*places, c * span, (1 - c) * span]).astype(jnp.int32)

    runs_of = [((2, 0, span),)]
    for first, count in chunks:
        runs_of.append(tuple((index, first * HD, count * HD) for index in (0, 1)))
    wide = [sum(size for _, _, size in runs) for runs in runs_of]
    lows = [sum(wide[:i]) for i in range(len(wide))]

    found = other_core(pack((keys, values, queries), sum(runs_of, ())))
    sent = [
        lax.dynamic_slice(out_weight, (0, lax.rem(x + d, n_head) * width + piece * block), (2 * span, block))
        for d in range(1, n_head)
    ]
    cuts = list(zip(lows, runs_of))
    message = join((keys, values), found, span, cuts[1:2])
    queries, *late = join((keys, values, queries), found, span, [cuts[0], *cuts[2:]])
    message = [*message, *late]
    near = [to_neighbours(message[0])]
    lists = jnp.concatenate([lists, other_core(lists)], axis=0)
    scalars = (jnp.stack(tiles).astype(jnp.int32), lists)

    near.append(to_neighbours(message[1]))
    crossed = [lax.ppermute(a, "head", ring(n_head, d + 1)) for d, a in enumerate(sent)]

    def runs(some):
        return [
            (index, side * chunks[i][1] * HD, splits + side, chunks[i][0] * HD, chunks[i][1] * HD)
            for index, i in enumerate(some)
            for side in (0, 1)
        ]

    def plan_of(i, sources):
        count = chunks[i][1]
        return [tuple((a, row, h * HD, (count + h) * HD) for a, row in sources) for h in range(count)]

    plan = sum((plan_of(i, ((i, 0), (i, rows))) for i in range(len(chunks))), [])
    prior = attend(0, plan, 0, scalars, queries, message)
    mine = lax.dynamic_slice(after(out_weight, prior), (0, x * width), (2 * span, width))
    near[0], crossed = lax.optimization_barrier((after(near[0], prior, mine), crossed))
    spread = [
        [got] + [lax.ppermute(got, "groups", ring(n_groups, n_groups - e)) for e in range(1, n_groups)]
        if splits > 1
        else [got]
        for got in crossed
    ]

    ours, moved = [], []
    for i, (first, _) in enumerate(chunks):
        plan = plan_of(i, [(index, row) for index in (0, 1) for row in (0, rows)])
        kept, given = attend(first, plan, 2, scalars, queries, near[i], prior)
        if i == last:
            break
        ours.append(jnp.concatenate([kept, other_core(given)], axis=1))
        leaving = after(ours[i], moved) if i else ours[i]
        moved.append([lax.ppermute(leaving, "head", ring(n_head, d)) for d in range(1, n_head)])
        if i + 2 < len(chunks):
            near.append(to_neighbours(after(message[i + 2], kept)))
        if i == 0:
            near[1] = after(near[1], kept, ours[0])
        if i == last - 1:
            (total,) = project(places, splits, [(runs(range(last)), ours, [mine], True)], width)
            near[last], spread = lax.optimization_barrier((after(near[last], total, moved), spread))
    pieces = [[a for got in gots for a in (got, other_core(got))] if splits > 1 else gots for gots in spread]

    parts = []
    for d in range(1, n_head):
        across = [(h * subs + s, ((h + d) % n_head) * subs + 1 - s) for h in range(n_head) for s in range(subs)]
        parts += [lax.ppermute(kept, "head", ring(n_head, d)), lax.ppermute(given, ("head", "sub"), across)]
    late = [(side, 0, splits + side, chunks[last][0] * HD, chunks[last][1] * HD) for side in (0, 1)]
    groups = [(late, [kept, other_core(given)], [mine], True)]
    groups += [(runs(range(last)), [moved[i][d] for i in range(last)], pieces[d], False) for d in range(n_head - 1)]
    total, weights = project(places, splits, groups, width, total, [late_run[2:] for late_run in late])
    return close(total, weights, parts, gate.reshape(1, width))


def solution(mesh):
    return jax.shard_map(
        local,
        mesh=mesh,
        in_specs=(
            P(("groups", "seq", "sub"), "head"),
            P(("groups", "seq", "sub"), "head"),
            P(("groups", "seq", "sub"), "head"),
            P(("groups", "seq", "sub"), None),
            P(("groups", "seq", "sub")),
            P("head", None),
            P("head"),
        ),
        out_specs=P(("groups", "seq", "sub"), "head"),
        check_vma=False,
    )
```

```python
import functools
import math

import jax
import jax.numpy as jnp
from jax import lax
from jax.experimental import pallas as pl
from jax.experimental.pallas import tpu as pltpu
from jax.sharding import PartitionSpec as P

HD = 128
LOG2E = 1.4426950408889634
FAR = 1e30
KERNEL_BYTES = 10 * 2**20
PROJECT_BYTES = 6 * 2**20
PACK_BYTES = 56 * 2**20
SHARES = (2, 2, 2)
SMEM_SPEC = pl.BlockSpec(memory_space=pltpu.SMEM)
VMEM_SPEC = pl.BlockSpec(memory_space=pltpu.VMEM)
HBM_SPEC = pl.BlockSpec(memory_space=pltpu.HBM)


def head_chunks(heads):
    whole = sum(SHARES)
    edges = sorted({(sum(SHARES[:i]) * heads) // whole for i in range(len(SHARES) + 1)})
    return [(low, high - low) for low, high in zip(edges[:-1], edges[1:])]


def pairing(length, first):
    pairs = [(i, i + 1) for i in range(first, length - 1, 2)]
    return pairs + [(b, a) for a, b in pairs]


def ring(length, distance):
    return [(i, (i + distance) % length) for i in range(length)]


def other_core(block):
    return lax.ppermute(block, "sub", [(0, 1), (1, 0)])


def to_neighbours(block):
    length = lax.axis_size("seq")
    return [lax.ppermute(block, "seq", pairing(length, start)) for start in (0, 1)]


def after(value, *earlier):
    return lax.optimization_barrier((value, *earlier))[0]


def pack_kernel(inputs, cuts, *refs):
    operands, outs, helds, sems = refs[:inputs], refs[inputs : inputs + len(cuts)], refs[inputs + len(cuts) : -1], refs[-1]
    arriving, leaving = [], []
    other_half = (1 - lax.axis_index("sub")) * (operands[0].shape[1] // 2)
    for runs, out, held in zip(cuts, outs, helds):
        at = 0
        for index, offset, width in runs:
            for step in range(0, width, HD):
                n = len(arriving)
                start = pl.multiple_of(other_half + (offset + step), HD)
                place = (slice(None), slice(at, at + HD))
                arriving.append(
                    pltpu.make_async_copy(operands[index].at[:, pl.ds(start, HD)], held.at[place], sems.at[0, n])
                )
                leaving.append(pltpu.make_async_copy(held.at[place], out.at[place], sems.at[1, n]))
                at += HD
    for copy in arriving:
        copy.start()
    for arrival, departure in zip(arriving, leaving):
        arrival.wait()
        departure.start()
    for copy in leaving:
        copy.wait()


def pack(operands, cuts):
    rows = operands[0].shape[0]
    shapes = [(rows, sum(width for _, _, width in runs)) for runs in cuts]
    copies = sum(width for _, width in shapes) // HD
    return pl.pallas_call(
        functools.partial(pack_kernel, len(operands), cuts),
        in_specs=[HBM_SPEC] * len(operands),
        out_specs=[HBM_SPEC] * len(cuts),
        out_shape=[jax.ShapeDtypeStruct(shape, jnp.bfloat16) for shape in shapes],
        scratch_shapes=[pltpu.VMEM(shape, jnp.bfloat16) for shape in shapes] + [pltpu.SemaphoreType.DMA((2, copies))],
        compiler_params=pltpu.CompilerParams(vmem_limit_bytes=PACK_BYTES),
    )(*operands)


def join_kernel(span, cuts, *refs):
    *operands, found = refs[: -len(cuts)]
    half = lax.axis_index("sub") * span
    for (low, runs), out in zip(cuts, refs[-len(cuts) :]):
        rows, width = found.shape[0], out.shape[1]
        at = 0
        for index, offset, size in runs:
            start = pl.multiple_of(half + offset, HD)
            out[:rows, at : at + size] = operands[index][:, pl.ds(start, size)]
            at += size
        out[rows:, :] = found[:, low : low + width]


def join(operands, found, span, cuts):
    rows = found.shape[0]
    widths = [sum(size for _, _, size in runs) for _, runs in cuts]
    return pl.pallas_call(
        functools.partial(join_kernel, span, cuts),
        in_specs=[VMEM_SPEC] * (len(operands) + 1),
        out_specs=[VMEM_SPEC] * len(cuts),
        out_shape=[jax.ShapeDtypeStruct((2 * rows, width), found.dtype) for width in widths],
        compiler_params=pltpu.CompilerParams(vmem_limit_bytes=PROJECT_BYTES),
    )(*operands, found)


def attention_kernel(first, plan, base, merge, tiles_ref, lists_ref, queries, *refs):
    arrays = max(index for held in plan for index, *_ in held) + 1
    operands, refs = refs[:arrays], refs[arrays:]
    if merge:
        prior_ref, mass_ref, *outs = refs
    else:
        out, mass_ref = refs
    rows = queries.shape[0] // 2
    entries = lists_ref.shape[1] - 1
    scale = LOG2E / math.sqrt(HD)
    early = lax.broadcasted_iota(jnp.int32, (1, 2 * rows), 1) < rows

    def included(query, tile):
        found = False
        for j in range(entries):
            found = found | ((lists_ref[query, j] == tile) & (j < lists_ref[query, entries]))
        return (found & (tile >= 0)).astype(jnp.int32)

    flags = []
    for s in range(len(plan[0])):
        tile = tiles_ref[base + s]
        flags.append(jnp.where(early, included(0, tile), included(1, tile)) > 0)

    def block(index, row, column):
        return operands[index][row : row + rows, column : column + HD]

    def scores(head):
        query = queries[:, (first + head) * HD : (first + head + 1) * HD]
        return [
            lax.dot_general(
                block(index, row, key), query, (((1,), (1,)), ((), ())), preferred_element_type=jnp.float32
            )
            for index, row, key, _ in plan[head]
        ]

    def finish(head, logits):
        cols = slice(head * HD, (head + 1) * HD)
        seen = slice((first + head) * HD, (first + head + 1) * HD)
        peak = before = mass_ref[first + head : first + head + 1, :] if merge else None
        for flag, logit in zip(flags, logits):
            top = jnp.where(flag, jnp.max(logit, axis=0, keepdims=True) * scale, -FAR)
            peak = top if peak is None else jnp.maximum(peak, top)
        accum = total = None
        for (index, row, _, value), flag, logit in zip(plan[head], flags, logits):
            weights = jnp.exp2(logit * scale - jnp.where(flag, peak, FAR))
            mass = jnp.sum(weights, axis=0, keepdims=True)
            term = lax.dot_general(
                block(index, row, value),
                weights.astype(jnp.bfloat16),
                (((0,), (0,)), ((), ())),
                preferred_element_type=jnp.float32,
            )
            total = mass if total is None else total + mass
            accum = term if accum is None else accum + term
        if merge:
            share = jnp.exp2(before - peak)
            accum = accum + share * prior_ref[seen, :]
            total = total + share
            result = accum * (1.0 / total)
            for i, out_i in enumerate(outs):
                out_i[:, cols] = jnp.transpose(result[:, i * rows : (i + 1) * rows]).astype(out_i.dtype)
        else:
            out[cols, :] = accum * (1.0 / total)
            mass_ref[head : head + 1, :] = peak + jnp.log2(total)

    logits = scores(0)
    for head in range(len(plan)):
        following = scores(head + 1) if head + 1 < len(plan) else None
        finish(head, logits)
        logits = following


def attend(first, plan, base, scalars, queries, operands, prior=None):
    rows = queries.shape[0] // 2
    count = len(plan)
    merge = prior is not None
    if merge:
        shapes = [jax.ShapeDtypeStruct((rows, count * HD), jnp.bfloat16)] * 2
    else:
        shapes = [
            jax.ShapeDtypeStruct((count * HD, 2 * rows), jnp.float32),
            jax.ShapeDtypeStruct((-(-count // 8) * 8, 2 * rows), jnp.float32),
        ]
    operands = (queries, *operands, *(prior or ()))
    return pl.pallas_call(
        functools.partial(attention_kernel, first, plan, base, merge),
        in_specs=[SMEM_SPEC] * 2 + [VMEM_SPEC] * len(operands),
        out_specs=[VMEM_SPEC] * 2,
        out_shape=shapes,
        compiler_params=pltpu.CompilerParams(vmem_limit_bytes=KERNEL_BYTES),
    )(*scalars, *operands)


def project_kernel(splits, groups, carried, late, place_ref, *refs):
    refs = list(refs)
    weights_out = refs.pop() if late else None
    out = refs.pop()
    total_ref = refs.pop(0) if carried else None
    block = out.shape[1] // splits
    for j in range(splits):
        where = pl.ds(pl.multiple_of(place_ref[j] * block, HD), block)
        total = total_ref[:, where] if carried else None
        at = row = 0
        for runs, arrays, pieces in groups:
            weights = refs[at + arrays : at + arrays + max(pieces, 1)]
            for index, column, place, offset, depth in runs:
                rows = pl.ds(pl.multiple_of(place_ref[place] + offset, HD), depth)
                right = weights[j][rows, :] if pieces else weights[0][rows, where]
                left = refs[at + index][:, column : column + depth]
                term = jnp.dot(left, right, preferred_element_type=jnp.float32)
                total = term if total is None else total + term
            for place, offset, depth in late if pieces else ():
                rows = pl.ds(pl.multiple_of(place_ref[place] + offset, HD), depth)
                weights_out[row : row + depth, where] = weights[j][rows, :]
                row += depth
            at += arrays + max(pieces, 1)
        out[:, where] = total


def project(places, splits, groups, width, total=None, late=()):
    operands = [] if total is None else [total]
    plan = []
    for runs, arrays, weights, whole in groups:
        plan.append((runs, len(arrays), 0 if whole else len(weights)))
        operands += [*arrays, *weights]
    rows = groups[0][1][0].shape[0]
    shapes = [jax.ShapeDtypeStruct((rows, width), jnp.float32)]
    if late:
        depth = sum(depth for _, _, depth in late) * sum(not whole for *_, whole in groups)
        shapes.append(jax.ShapeDtypeStruct((depth, width), jnp.bfloat16))
    return pl.pallas_call(
        functools.partial(project_kernel, splits, plan, total is not None, late),
        in_specs=[SMEM_SPEC] + [VMEM_SPEC] * len(operands),
        out_specs=[VMEM_SPEC] * len(shapes),
        out_shape=shapes,
        compiler_params=pltpu.CompilerParams(vmem_limit_bytes=PROJECT_BYTES),
    )(places, *operands)


def close_kernel(blocks, total_ref, weights_ref, gate_ref, *refs):
    *parts, out, held, sems = refs
    block = out.shape[1] // blocks
    copies = []
    for j in range(blocks):
        where = slice(j * block, (j + 1) * block)
        total = total_ref[:, where]
        row = 0
        for part in parts:
            depth = part.shape[1]
            right = weights_ref[row : row + depth, where]
            total = total + jnp.dot(part[...], right, preferred_element_type=jnp.float32)
            row += depth
        held[:, where] = (total * gate_ref[:, where]).astype(out.dtype)
        copies.append(pltpu.make_async_copy(held.at[:, where], out.at[:, where], sems.at[j]))
        copies[-1].start()
    for copy in copies:
        copy.wait()


def close(total, weights, parts, gate):
    rows, width = total.shape
    blocks = max(width // (4 * HD), 1)
    return pl.pallas_call(
        functools.partial(close_kernel, blocks),
        in_specs=[VMEM_SPEC] * (3 + len(parts)),
        out_specs=HBM_SPEC,
        out_shape=jax.ShapeDtypeStruct((rows, width), jnp.bfloat16),
        scratch_shapes=[pltpu.VMEM((rows, width), jnp.bfloat16), pltpu.SemaphoreType.DMA((blocks,))],
        compiler_params=pltpu.CompilerParams(vmem_limit_bytes=PROJECT_BYTES),
    )(total, weights, gate, *parts)


def local(queries, keys, values, kv_list, kv_count, out_weight, gate):
    rows = queries.shape[0]
    length, subs = lax.axis_size("seq"), lax.axis_size("sub")
    n_head, n_groups = lax.axis_size("head"), lax.axis_size("groups")
    z, c = lax.axis_index("seq"), lax.axis_index("sub")
    x, g = lax.axis_index("head"), lax.axis_index("groups")
    width = out_weight.shape[1] // n_head
    heads = queries.shape[1] // HD
    if heads % 2:
        queries, keys, values = (jnp.pad(a, ((0, 0), (0, HD))) for a in (queries, keys, values))
        out_weight = jnp.pad(out_weight, ((0, HD), (0, 0)))
    half = (heads + 1) // 2
    span = half * HD
    chunks = head_chunks(half)
    last = len(chunks) - 1

    even = z + 1 - 2 * lax.rem(z, 2)
    odd = z - 1 + 2 * lax.rem(z, 2)
    tiles = []
    for place in (z, even, odd):
        inside = (place >= 0) & (place < length)
        tiles += [jnp.where(inside, place * subs + c, -1), jnp.where(inside, place * subs + 1 - c, -1)]
    lists = jnp.concatenate([kv_list, kv_count.reshape(1, 1)], axis=1)

    splits = n_groups * subs
    if width % (splits * HD):
        splits = 1
    block = width // splits
    if splits > 1:
        places = [lax.rem(g + d, n_groups) * subs + s for d in range(n_groups) for s in (c, 1 - c)]
    else:
        places = [0]

    def piece_at(d):
        there = lax.rem(lax.axis_index("head") + d, n_head) * width
        return there + ((lax.axis_index("groups") * subs + lax.axis_index("sub")) * block if splits > 1 else 0)

    piece = places[0]
    places = jnp.stack([*places, c * span, (1 - c) * span]).astype(jnp.int32)

    runs_of = [((2, 0, span),)]
    for first, count in chunks:
        runs_of.append(tuple((index, first * HD, count * HD) for index in (0, 1)))
    wide = [sum(size for _, _, size in runs) for runs in runs_of]
    lows = [0] + [sum(wide[1:i]) for i in range(1, len(wide))]

    found, found_queries = (
        other_core(packed) for packed in pack((keys, values, queries), (sum(runs_of[1:], ()), runs_of[0]))
    )
    sent = [
        lax.dynamic_slice(out_weight, (0, lax.rem(x + d, n_head) * width + piece * block), (2 * span, block))
        for d in range(1, n_head)
    ]
    cuts = list(zip(lows, runs_of))
    message = join((keys, values), found, span, cuts[1:2])
    message += join((keys, values), found, span, cuts[2:])
    (queries,) = join((queries,), found_queries, span, [(0, ((0, 0, span),))])
    near = [to_neighbours(message[0])]
    lists = jnp.concatenate([lists, other_core(lists)], axis=0)
    scalars = (jnp.stack(tiles).astype(jnp.int32), lists)

    near.append(to_neighbours(message[1]))
    crossed = [lax.ppermute(a, "head", ring(n_head, d + 1)) for d, a in enumerate(sent)]

    def runs(some):
        return [
            (index, side * chunks[i][1] * HD, splits + side, chunks[i][0] * HD, chunks[i][1] * HD)
            for index, i in enumerate(some)
            for side in (0, 1)
        ]

    def plan_of(i, sources):
        count = chunks[i][1]
        return [tuple((a, row, h * HD, (count + h) * HD) for a, row in sources) for h in range(count)]

    plan = sum((plan_of(i, ((i, 0), (i, rows))) for i in range(len(chunks))), [])
    prior = attend(0, plan, 0, scalars, queries, message)
    mine = lax.dynamic_slice(after(out_weight, prior), (0, x * width), (2 * span, width))
    near[0], crossed = lax.optimization_barrier((after(near[0], prior, mine), crossed))
    spread = [
        [got] + [lax.ppermute(got, "groups", ring(n_groups, n_groups - e)) for e in range(1, n_groups)]
        if splits > 1
        else [got]
        for got in crossed
    ]

    ours, moved = [], []
    for i, (first, _) in enumerate(chunks):
        plan = plan_of(i, [(index, row) for index in (0, 1) for row in (0, rows)])
        kept, given = attend(first, plan, 2, scalars, queries, near[i], prior)
        if i == last:
            break
        ours.append(jnp.concatenate([kept, other_core(given)], axis=1))
        leaving = after(ours[i], moved) if i else ours[i]
        moved.append([lax.ppermute(leaving, "head", ring(n_head, d)) for d in range(1, n_head)])
        if i + 2 < len(chunks):
            near.append(to_neighbours(after(message[i + 2], kept)))
        if i == 0:
            near[1] = after(near[1], kept, ours[0])
        if i == last - 1:
            (total,) = project(places, splits, [(runs(range(last)), ours, [mine], True)], width)
            near[last], spread = lax.optimization_barrier((after(near[last], total, moved), spread))
    pieces = [[a for got in gots for a in (got, other_core(got))] if splits > 1 else gots for gots in spread]

    parts = []
    for d in range(1, n_head):
        across = [(h * subs + s, ((h + d) % n_head) * subs + 1 - s) for h in range(n_head) for s in range(subs)]
        parts += [lax.ppermute(kept, "head", ring(n_head, d)), lax.ppermute(given, ("head", "sub"), across)]
    late = [(side, 0, splits + side, chunks[last][0] * HD, chunks[last][1] * HD) for side in (0, 1)]
    groups = [(late, [kept, other_core(given)], [mine], True)]
    groups += [(runs(range(last)), [moved[i][d] for i in range(last)], pieces[d], False) for d in range(n_head - 1)]
    total, weights = project(places, splits, groups, width, total, [late_run[2:] for late_run in late])
    return close(total, weights, parts, gate.reshape(1, width))


def solution(mesh):
    return jax.shard_map(
        local,
        mesh=mesh,
        in_specs=(
            P(("groups", "seq", "sub"), "head"),
            P(("groups", "seq", "sub"), "head"),
            P(("groups", "seq", "sub"), "head"),
            P(("groups", "seq", "sub"), None),
            P(("groups", "seq", "sub")),
            P("head", None),
            P("head"),
        ),
        out_specs=P(("groups", "seq", "sub"), "head"),
        check_vma=False,
    )
```
